512 devices in a mesh: freq: 128 (over y, z, core), rows: 4 (over x).
Axes of the slice: x: 4, y: 8, z: 8, core: 2. Of those that a mesh axis runs over, the one named last changes fastest.
Arguments:
- direct: float32 [96, 1536, 256], P('rows', 'freq'), may hold values from -6 to 6
- current: float32 [96, 1536, 256], P('rows', 'freq'), may hold values from -6 to 6
- onsets: int32 [96, 1536], P('rows', 'freq'), may hold values from 32 to 128
- reflection: bfloat16 [2, 128, 1536, 1536], P(None, 'freq', None, 'rows'), may hold values from -0.15625 to 0.15625
Outputs:
- upgoing: float32 [96, 1536, 256], P('rows', 'freq')
- downgoing: float32 [96, 1536, 256], P('rows', 'freq')
The draws below stay inside these ranges and needn't reach their ends.
All inputs are finite; a program needn't handle non-finite values.
Results may differ from the reference program's by a relative error of at most 0.0031.
Values may be sent and summed in bfloat16 or wider, within the bound.
A program may use at most 64 MiB of HBM per device.

```python
import math
import jax
import jax.numpy as jnp
from jax import lax

NREC = 1536
FP = 96
NF = 128
NT = 256


def plant(drawn, own_key, least, high):
    spot = [jax.random.randint(jax.random.fold_in(own_key, axis), (), 0, length) for axis, length in enumerate(drawn.shape)]
    widest = drawn.shape.index(max(drawn.shape))
    next_to = spot[:widest] + [(spot[widest] + 1) % drawn.shape[widest]] + spot[widest + 1:]
    return drawn.at[tuple(spot)].set(least).at[tuple(next_to)].set(high)


def block_scale(stream_key, extent, pieces, low, largest):
    factor_of, own = 1.0, jax.random.fold_in(stream_key, 6)
    for axis_at, blocks in pieces:
        steps = jnp.exp(jax.random.uniform(jax.random.fold_in(own, axis_at), (blocks,), jnp.float32, low / len(pieces), largest / len(pieces)))
        factor_of = factor_of * jnp.repeat(steps, extent[axis_at] // blocks).reshape([-1 if axis == axis_at else 1 for axis in range(len(extent))])
    return factor_of


def bell_draw(rng, dims, spread, limit, split=(), held_as=jnp.bfloat16):
    entries = jax.random.normal(rng, dims, jnp.float32) * spread
    if len(split) > 0:
        entries = block_scale(rng, dims, split, -0.22, 0.18) * entries
    return jnp.clip(entries, min=-limit, max=limit).astype(held_as)


def setup_inputs(seed: int = 0) -> dict:
    streams_of = jax.random.split(jax.random.key(seed), 5)
    return {
        "direct": bell_draw(streams_of[0], (FP, NREC, NT), 1.0, 6.0, ((0, 4), (1, 128)), jnp.float32),
        "current": bell_draw(streams_of[1], (FP, NREC, NT), 1.0, 6.0, ((0, 4), (1, 128)), jnp.float32),
        "onsets": plant(jax.random.randint(streams_of[2], (FP, NREC), NT // 8, NT // 2 + 1), jax.random.fold_in(streams_of[2], 1), NT // 8, (NT // 2 + 1) - 1).astype(jnp.int32),
        "reflection": bell_draw(streams_of[3], (2, NF, NREC, NREC), NREC ** -0.5, 0.15625, ((1, 128), (3, 4))),
    }


def tables(nfreq, ntime):
    freqs = jnp.arange(nfreq).astype(jnp.int32)[:, None]
    times = jnp.arange(ntime).astype(jnp.int32)[None, :]
    phase = ((freqs * times) % ntime).astype(jnp.float32) * jnp.float32(2.0 * math.pi / ntime)
    cosine = jnp.cos(phase)
    sine = jnp.sin(phase)
    weights = jnp.where(freqs == 0, 1.0, 2.0).astype(jnp.float32) / jnp.float32(ntime)
    forward = jnp.stack([cosine, -sine])
    inverse = jnp.stack([weights * cosine, -weights * sine])
    return forward, inverse


def reference(direct, current, onsets, reflection):
    forward, inverse = tables(NF, NT)
    samples = jnp.arange(NT).astype(jnp.int32)
    starts = onsets[:, :, None]
    window = ((samples < starts) | (samples > NT - starts)).astype(jnp.float32)

    def to_freq(field):
        return jnp.einsum("ckt,prt->ckpr", forward, field, precision=lax.Precision.HIGHEST).astype(jnp.bfloat16)

    def to_time(spectrum):
        return jnp.einsum("ckt,ckpr->prt", inverse, spectrum, precision=lax.Precision.HIGHEST)

    spec_down = to_freq(current)

    def apply_forward(index):
        real_r = reflection[0, index]
        imag_r = reflection[1, index]
        real_s = spec_down[0, index]
        imag_s = spec_down[1, index]
        real_p = jnp.dot(real_s, real_r.T, preferred_element_type=jnp.float32) - jnp.dot(imag_s, imag_r.T, preferred_element_type=jnp.float32)
        imag_p = jnp.dot(real_s, imag_r.T, preferred_element_type=jnp.float32) + jnp.dot(imag_s, real_r.T, preferred_element_type=jnp.float32)
        return jnp.stack([real_p, imag_p])

    prod_up = lax.map(apply_forward, jnp.arange(NF).astype(jnp.int32)).transpose(1, 0, 2, 3)
    upgoing = to_time(prod_up) * window
    spec_up = to_freq(upgoing)

    def apply_back(index):
        real_r = reflection[0, index]
        imag_r = reflection[1, index]
        real_x = spec_up[0, index]
        imag_x = spec_up[1, index]
        real_p = jnp.dot(real_x, real_r, preferred_element_type=jnp.float32) + jnp.dot(imag_x, imag_r, preferred_element_type=jnp.float32)
        imag_p = jnp.dot(imag_x, real_r, preferred_element_type=jnp.float32) - jnp.dot(real_x, imag_r, preferred_element_type=jnp.float32)
        return jnp.stack([real_p, imag_p])

    prod_down = lax.map(apply_back, jnp.arange(NF).astype(jnp.int32)).transpose(1, 0, 2, 3)
    downgoing = direct + to_time(prod_down) * window
    return upgoing, downgoing
```

```python
import functools
import math

import jax
import jax.numpy as jnp
import ml_dtypes
import numpy as np
from jax import lax
from jax.experimental import pallas as pl
from jax.experimental.pallas import tpu as pltpu
from jax.sharding import PartitionSpec as P

MESH = pl.DeviceIdType.MESH
PAD = 32
TILE = 128
PEAK = 32000.0
SPOT = 31
F32, BF16, I16 = jnp.float32, jnp.bfloat16, jnp.int16


def split(table):
    high = table.astype(ml_dtypes.bfloat16)
    low = (table - high.astype(np.float64)).astype(ml_dtypes.bfloat16)
    return np.stack([high, low])


def tables(nfreq, ntime):
    phase = (np.arange(nfreq)[:, None] * np.arange(ntime)[None, :] % ntime) * (2.0 * math.pi / ntime)
    weights = np.where(np.arange(nfreq) == 0, 1.0, 2.0)[:, None] / ntime
    forward = np.stack([np.cos(phase), -np.sin(phase)], axis=1)
    inverse = forward * weights[:, None]
    return (
        split(forward.reshape(2 * nfreq, ntime)),
        split(inverse.reshape(2 * nfreq, ntime)),
    )


def halves(value):
    high = value.astype(BF16)
    return high, (value - high.astype(F32)).astype(BF16)


def dot(a, b, contract):
    return lax.dot_general(a, b, (contract, ((), ())), preferred_element_type=F32)


def swap_blocks(arrays):
    shape = arrays[0].shape
    block = lax.broadcasted_iota(jnp.int32, shape, len(shape) - 1) // PAD
    low, even = block < 2, block % 2 == 0
    a0, a1, a2, a3 = arrays
    turn = lambda a, shift: pltpu.roll(a, shift, len(shape) - 1)
    b0, b2 = jnp.where(low, a0, turn(a2, 64)), jnp.where(low, turn(a0, 64), a2)
    b1, b3 = jnp.where(low, a1, turn(a3, 64)), jnp.where(low, turn(a1, 64), a3)
    c0, c1 = jnp.where(even, b0, turn(b1, 32)), jnp.where(even, turn(b0, 96), b1)
    c2, c3 = jnp.where(even, b2, turn(b3, 32)), jnp.where(even, turn(b2, 96), b3)
    return [c0, c1, c2, c3]


def encode(value):
    lane = lax.broadcasted_iota(jnp.int32, value.shape, 1)
    largest = jnp.max(jnp.abs(value), axis=1, keepdims=True)
    power = jnp.ceil(jnp.log2(jnp.maximum(largest, 1e-30)) + 1e-3)
    codes = jnp.round(value * (jnp.exp2(-power) * PEAK))
    return jnp.where(lane == SPOT, power, codes).astype(jnp.int32).astype(I16)


def decode(codes):
    codes = codes.astype(jnp.int32).astype(F32)
    return codes * (jnp.exp2(codes[:, SPOT : SPOT + 1]) * (1.0 / PEAK))


def kernel(
    dims,
    direct_hbm, current_hbm, onsets_ref, reflection_hbm, forward_hbm, inverse_hbm,
    up_ref, down_ref,
    direct_ref, current_ref, refl, back, forward_ref, inverse_ref, field,
    send_a, got_a, cols_a, stage, weights,
    partial, blocks, send_s, got_s, send_b, got_b,
    send_c, got_c, all_c, full, product,
    send_e, got_e, got_d,
    load_sem, send_sem, recv_sem,
):
    nf, nx, nr, npt = dims
    nb = nf // nx
    rows = 2 * nf
    wide = nr * PAD
    f, x = lax.axis_index("freq"), lax.axis_index("rows")

    loads = [
        pltpu.make_async_copy(source, target, load_sem.at[i])
        for i, (source, target) in enumerate(
            [
                (current_hbm, current_ref),
                (forward_hbm, forward_ref),
                (reflection_hbm, refl),
                (inverse_hbm, inverse_ref),
                (direct_hbm, direct_ref),
            ]
        )
    ]
    for load in loads:
        load.start()

    barrier = pltpu.get_barrier_semaphore()

    def greet(step, carry):
        pl.semaphore_signal(barrier, inc=1, device_id=(lax.rem(f + step, nf), x), device_id_type=MESH)
        return carry

    lax.fori_loop(1, nf, greet, 0)
    for step in range(1, nx):
        pl.semaphore_signal(barrier, inc=1, device_id=(f, lax.rem(x + step, nx)), device_id_type=MESH)

    def exchange(source, target, which):
        def one(step, carry):
            peer = lax.rem(f + step, nf)
            pltpu.make_async_remote_copy(
                src_ref=source.at[peer], dst_ref=target.at[f],
                send_sem=send_sem.at[which], recv_sem=recv_sem.at[which],
                device_id=(peer, x), device_id_type=MESH,
            ).start()
            return carry

        lax.fori_loop(1, nf, one, 0, unroll=min(8, nf - 1))
        target[f] = source[f]

    def finish(source, target, which, count):
        pltpu.make_async_copy(source.at[pl.ds(0, count)], source.at[pl.ds(0, count)], send_sem.at[which]).wait()
        pltpu.make_async_copy(target.at[pl.ds(0, count)], target.at[pl.ds(0, count)], recv_sem.at[which]).wait()

    def to_rows(pick, target, which):
        for step in range(1, nx):
            peer = lax.rem(x + step, nx)
            pltpu.make_async_remote_copy(
                src_ref=pick(peer), dst_ref=target.at[x],
                send_sem=send_sem.at[which], recv_sem=recv_sem.at[which],
                device_id=(f, peer), device_id_type=MESH,
            ).start()

    def transform():
        high, low = halves(field[...])
        spectra = (
            dot(forward_ref[0], high, ((1,), (1,)))
            + dot(forward_ref[0], low, ((1,), (1,)))
            + dot(forward_ref[1], high, ((1,), (1,)))
        )
        return spectra.astype(BF16).reshape(nf, 2, wide)

    def invert(messages):
        high, low = halves(decode(messages.reshape(rows, wide)))
        return (
            dot(high, inverse_ref[0], ((0,), (0,)))
            + dot(low, inverse_ref[0], ((0,), (0,)))
            + dot(high, inverse_ref[1], ((0,), (0,)))
        )

    samples = lax.broadcasted_iota(jnp.int32, (npt, 2 * nf), 1)

    def window(r):
        start = onsets_ref[:, r : r + 1]
        return (samples < start) | (samples > 2 * nf - start)

    field[...] = jnp.zeros_like(field)
    loads[0].wait()
    for r in range(nr):
        field[r * PAD : r * PAD + npt, :] = current_ref[:, r, :]
    loads[1].wait()
    send_a[...] = transform()
    pl.semaphore_wait(barrier, nf - 1 + nx - 1)
    exchange(send_a, got_a, 0)
    loads[2].wait()
    for c in range(2):
        back[c] = jnp.swapaxes(refl[c], 0, 1)
    finish(send_a, got_a, 0, nf - 1)

    to_rows(lambda peer: got_a.at[pl.ds(peer * nb, nb)], cols_a, 1)
    cols_a[x] = got_a[pl.ds(x * nb, nb)]
    finish(cols_a, cols_a, 1, nx - 1)

    def spread(messages, count, target):
        for i in range(nx):
            message = messages(i).reshape(2 * count, wide).astype(F32)
            for t in range(nr // 4):
                stage[i, t, : 2 * count] = message[:, t * TILE : (t + 1) * TILE]
        for t in range(nr // 4):
            for c in range(2):
                parts = swap_blocks(
                    [stage[i, t, pl.ds(c, count, stride=2), :] for i in range(nx)]
                )
                for j in range(4):
                    target[c, pl.ds(4 * t + j, count, stride=nr), :] = parts[j]

    def gather(source, count, target):
        for t in range(nr // 4):
            for c in range(2):
                parts = swap_blocks(
                    [source[c, pl.ds(4 * t + j, count, stride=nr), :] for j in range(4)]
                )
                for i in range(nx):
                    target[i, t, pl.ds(c, count, stride=2), :] = parts[i]

    def joined(source, i, count):
        return jnp.concatenate([source[i, t, :count] for t in range(nr // 4)], axis=1)

    spread(lambda i: cols_a[i], nb, weights)
    real, imag = weights[0].astype(BF16), weights[1].astype(BF16)
    sums = dot(refl[0], jnp.concatenate([real, imag], axis=1), ((1,), (0,))) + dot(
        refl[1], jnp.concatenate([-imag, real], axis=1), ((1,), (0,))
    )
    partial[0], partial[1] = sums[:, :TILE], sums[:, TILE:]
    gather(partial, nf, blocks)
    for i in range(nx):
        send_s[i] = encode(joined(blocks, i, rows))
    to_rows(lambda peer: send_s.at[peer], got_s, 2)
    finish(send_s, got_s, 2, nx - 1)
    total = joined(blocks, x, rows)
    for step in range(1, nx):
        total = total + decode(got_s[lax.rem(x + step, nx)])

    send_b[...] = encode(total).reshape(nf, 2, wide)
    exchange(send_b, got_b, 3)
    loads[3].wait()
    finish(send_b, got_b, 3, nf - 1)
    signal = invert(got_b[...])
    for r in range(nr):
        kept = jnp.where(window(r), signal[r * PAD : r * PAD + npt], 0.0)
        up_ref[:, r, :] = kept
        field[r * PAD : r * PAD + npt, :] = kept

    send_c[...] = transform()
    exchange(send_c, got_c, 4)
    finish(send_c, got_c, 4, nf - 1)
    to_rows(lambda peer: got_c, all_c, 5)
    all_c[x] = got_c[...]
    finish(all_c, all_c, 5, nx - 1)

    spread(lambda i: all_c[i], nf, full)
    real, imag = full[0].astype(BF16), full[1].astype(BF16)
    sums = dot(back[0], jnp.concatenate([real, imag], axis=1), ((1,), (0,))) + dot(
        back[1], jnp.concatenate([imag, -real], axis=1), ((1,), (0,))
    )
    product[0], product[1] = sums[:, :TILE], sums[:, TILE:]
    gather(product, nb, stage)
    for i in range(nx):
        send_e[i] = encode(joined(stage, i, 2 * nb)).reshape(nb, 2, wide)
    to_rows(lambda peer: send_e.at[peer], got_e, 6)
    got_e[x] = send_e[x]
    finish(send_e, got_e, 6, nx - 1)

    def last(step, carry):
        peer = lax.rem(f + step, nf)
        pltpu.make_async_remote_copy(
            src_ref=got_e.at[peer // nb, lax.rem(peer, nb)], dst_ref=got_d.at[f],
            send_sem=send_sem.at[7], recv_sem=recv_sem.at[7],
            device_id=(peer, x), device_id_type=MESH,
        ).start()
        return carry

    lax.fori_loop(1, nf, last, 0, unroll=min(8, nf - 1))
    got_d[f] = got_e[f // nb, lax.rem(f, nb)]
    loads[4].wait()
    finish(send_c, got_d, 7, nf - 1)
    signal = invert(got_d[...])
    for r in range(nr):
        kept = jnp.where(window(r), signal[r * PAD : r * PAD + npt], 0.0)
        down_ref[:, r, :] = direct_ref[:, r, :] + kept


def shards(nf, nx, direct, current, onsets, reflection):
    npt, nr, ntime = current.shape
    nb, wide = nf // nx, nr * PAD
    sources, columns = nf * nr, nb * nr
    forward, inverse = tables(nf, ntime)
    reflection = reflection.reshape(2, sources, columns)
    vmem = lambda shape, dtype: pltpu.VMEM(shape, dtype)
    scratch = [
        vmem((npt, nr, ntime), F32),
        vmem((npt, nr, ntime), F32),
        vmem((2, sources, columns), BF16),
        vmem((2, columns, sources), BF16),
        vmem((2, 2 * nf, ntime), BF16),
        vmem((2, 2 * nf, ntime), BF16),
        vmem((wide, ntime), F32),
        vmem((nf, 2, wide), BF16),
        vmem((nf, 2, wide), BF16),
        vmem((nx, nb, 2, wide), BF16),
        vmem((nx, nr // 4, 2 * nf, TILE), F32),
        vmem((2, columns, TILE), F32),
        vmem((2, sources, TILE), F32),
        vmem((nx, nr // 4, 2 * nf, TILE), F32),
        vmem((nx, 2 * nf, wide), I16),
        vmem((nx, 2 * nf, wide), I16),
        vmem((nf, 2, wide), I16),
        vmem((nf, 2, wide), I16),
        vmem((nf, 2, wide), BF16),
        vmem((nf, 2, wide), BF16),
        vmem((nx, nf, 2, wide), BF16),
        vmem((2, sources, TILE), F32),
        vmem((2, columns, TILE), F32),
        vmem((nx, nb, 2, wide), I16),
        vmem((nx, nb, 2, wide), I16),
        vmem((nf, 2, wide), I16),
        pltpu.SemaphoreType.DMA((5,)),
        pltpu.SemaphoreType.DMA((8,)),
        pltpu.SemaphoreType.DMA((8,)),
    ]
    hbm, inside = pl.BlockSpec(memory_space=pl.ANY), pl.BlockSpec(memory_space=pltpu.VMEM)
    out = jax.ShapeDtypeStruct((npt, nr, ntime), F32)
    return pl.pallas_call(
        functools.partial(kernel, (nf, nx, nr, npt)),
        out_shape=(out, out),
        in_specs=[hbm, hbm, inside, hbm, hbm, hbm],
        out_specs=(inside, inside),
        scratch_shapes=scratch,
        compiler_params=pltpu.CompilerParams(
            collective_id=0, has_side_effects=True, vmem_limit_bytes=48 * 1024 * 1024
        ),
        name="marchenko",
    )(direct, current, onsets, reflection, jnp.asarray(forward), jnp.asarray(inverse))


def solution(mesh):
    nf, nx = mesh.shape["freq"], mesh.shape["rows"]
    in_specs = (
        P("rows", "freq", None),
        P("rows", "freq", None),
        P("rows", "freq"),
        P(None, "freq", None, "rows"),
    )
    out_specs = (P("rows", "freq", None), P("rows", "freq", None))
    return jax.shard_map(
        functools.partial(shards, nf, nx), mesh=mesh, in_specs=in_specs, out_specs=out_specs, check_vma=False
    )
```

```python
import functools
import math

import jax
import jax.numpy as jnp
import ml_dtypes
import numpy as np
from jax import lax
from jax.experimental import pallas as pl
from jax.experimental.pallas import tpu as pltpu
from jax.sharding import PartitionSpec as P

MESH = pl.DeviceIdType.MESH
PAD = 32
TILE = 128
PEAK = 32000.0
SPOT = 31
F32, BF16, I16 = jnp.float32, jnp.bfloat16, jnp.int16


def split(table):
    high = table.astype(ml_dtypes.bfloat16)
    low = (table - high.astype(np.float64)).astype(ml_dtypes.bfloat16)
    return np.stack([high, low])


def tables(nfreq, ntime):
    phase = (np.arange(nfreq)[:, None] * np.arange(ntime)[None, :] % ntime) * (2.0 * math.pi / ntime)
    weights = np.where(np.arange(nfreq) == 0, 1.0, 2.0)[:, None] / ntime
    forward = np.stack([np.cos(phase), -np.sin(phase)], axis=1)
    inverse = forward * weights[:, None]
    return (
        split(forward.reshape(2 * nfreq, ntime)),
        split(inverse.reshape(2 * nfreq, ntime)),
    )


def halves(value):
    high = value.astype(BF16)
    return high, (value - high.astype(F32)).astype(BF16)


def dot(a, b, contract):
    return lax.dot_general(a, b, (contract, ((), ())), preferred_element_type=F32)


def swap_blocks(arrays):
    shape = arrays[0].shape
    block = lax.broadcasted_iota(jnp.int32, shape, len(shape) - 1) // PAD
    low, even = block < 2, block % 2 == 0
    a0, a1, a2, a3 = arrays
    turn = lambda a, shift: pltpu.roll(a, shift, len(shape) - 1)
    b0, b2 = jnp.where(low, a0, turn(a2, 64)), jnp.where(low, turn(a0, 64), a2)
    b1, b3 = jnp.where(low, a1, turn(a3, 64)), jnp.where(low, turn(a1, 64), a3)
    c0, c1 = jnp.where(even, b0, turn(b1, 32)), jnp.where(even, turn(b0, 96), b1)
    c2, c3 = jnp.where(even, b2, turn(b3, 32)), jnp.where(even, turn(b2, 96), b3)
    return [c0, c1, c2, c3]


def encode(value):
    lane = lax.broadcasted_iota(jnp.int32, value.shape, 1)
    largest = jnp.max(jnp.abs(value), axis=1, keepdims=True)
    power = jnp.ceil(jnp.log2(jnp.maximum(largest, 1e-30)) + 1e-3)
    codes = jnp.round(value * (jnp.exp2(-power) * PEAK))
    return jnp.where(lane == SPOT, power, codes).astype(jnp.int32).astype(I16)


def decode(codes):
    codes = codes.astype(jnp.int32).astype(F32)
    return codes * (jnp.exp2(codes[:, SPOT : SPOT + 1]) * (1.0 / PEAK))


def kernel(
    dims,
    direct_hbm, current_hbm, onsets_ref, reflection_hbm, forward_hbm, inverse_hbm,
    up_ref, down_ref,
    direct_ref, current_ref, refl, back, forward_ref, inverse_ref, field, window,
    send_a, got_a, cols_a, stage, weights,
    partial, blocks, send_s, got_s, send_b, got_b,
    send_c, got_c, all_c, full, product,
    send_e, got_e, got_d,
    load_sem, send_sem, recv_sem, recv_a, recv_s, recv_c, recv_g, recv_e,
):
    nf, nx, nr, npt = dims
    nb = nf // nx
    rows = 2 * nf
    wide = nr * PAD
    ny = 2 * nx
    nzc = nf // ny
    f, x = lax.axis_index("freq"), lax.axis_index("rows")
    y, zc = f // nzc, lax.rem(f, nzc)

    loads = [
        pltpu.make_async_copy(source, target, load_sem.at[i])
        for i, (source, target) in enumerate(
            [
                (current_hbm, current_ref),
                (forward_hbm, forward_ref),
                (reflection_hbm, refl),
                (inverse_hbm, inverse_ref),
                (direct_hbm, direct_ref),
            ]
        )
    ]
    for load in loads:
        load.start()

    def offset(count, i):
        if isinstance(i, int):
            return count // 2 + (i + 1) // 2 * (1 - 2 * (i % 2))
        return count // 2 + lax.div(i + 1, 2) * (1 - 2 * lax.rem(i, 2))

    def group(i):
        return lax.rem(y + offset(ny, i), ny)

    def members(row, act, own):
        for j in range(nzc - (not own)):
            act(row * nzc + lax.rem(zc + offset(nzc, j), nzc))

    def each_group(act):
        def one(i, carry):
            act(i, group(i), True)
            return carry

        lax.fori_loop(0, ny - 1, one, 0)
        act(ny - 1, y, False)

    def each_group_near(act):
        act(ny - 1, y, False)

        def one(i, carry):
            act(ny - 1 - i, group(ny - 1 - i), True)
            return carry

        lax.fori_loop(1, ny, one, 0)

    def part(row, size=None):
        size = nzc if size is None else size
        return pl.ds(pl.multiple_of(row * size, size), size)

    barrier = pltpu.get_barrier_semaphore()

    def greet(peer):
        pl.semaphore_signal(barrier, inc=1, device_id=(peer, x), device_id_type=MESH)

    each_group(lambda i, row, own: members(row, greet, own))
    for step in range(1, nx):
        pl.semaphore_signal(barrier, inc=1, device_id=(f, lax.rem(x + step, nx)), device_id_type=MESH)

    def message(source, target, send, recv, peer):
        pltpu.make_async_remote_copy(
            src_ref=source, dst_ref=target, send_sem=send, recv_sem=recv, device_id=peer, device_id_type=MESH
        ).start()

    def deliver(source, target, which, recv, row, own):
        members(
            row,
            lambda peer: message(source.at[peer], target.at[f], send_sem.at[which], recv, (peer, x)),
            own,
        )

    def arrived(ref, count, sem):
        pltpu.make_async_copy(ref.at[pl.ds(0, count)], ref.at[pl.ds(0, count)], sem).wait()

    def transform():
        high, low = halves(field[...])
        spectra = (
            dot(forward_ref[0], high, ((1,), (1,)))
            + dot(forward_ref[0], low, ((1,), (1,)))
            + dot(forward_ref[1], high, ((1,), (1,)))
        )
        return spectra.astype(BF16).reshape(nf, 2, wide)

    def invert(messages):
        high, low = halves(decode(messages.reshape(rows, wide)))
        return (
            dot(high, inverse_ref[0], ((0,), (0,)))
            + dot(low, inverse_ref[0], ((0,), (0,)))
            + dot(high, inverse_ref[1], ((0,), (0,)))
        )

    def fill_window():
        samples = lax.broadcasted_iota(jnp.int32, (npt, 2 * nf), 1).astype(F32)
        own = lax.broadcasted_iota(jnp.int32, (npt, npt), 0) == lax.broadcasted_iota(jnp.int32, (npt, npt), 1)
        window[...] = jnp.zeros_like(window)
        for r in range(nr):
            spread_out = jnp.where(own, onsets_ref[r : r + 1, :].astype(F32), 0.0)
            start = jnp.sum(spread_out, axis=1, keepdims=True)
            inside = (samples < start) | (samples > 2 * nf - start)
            window[r * PAD : r * PAD + npt, :] = jnp.where(inside, 1.0, 0.0)

    def spread(messages, count, target, g):
        for i in range(nx):
            rows_in = messages(i).reshape(2 * count, wide).astype(F32)
            for t in range(nr // 4):
                stage[i, t, : 2 * count] = rows_in[:, t * TILE : (t + 1) * TILE]
        for t in range(nr // 4):
            for c in range(2):
                parts = swap_blocks([stage[i, t, pl.ds(c, count, stride=2), :] for i in range(nx)])
                for j in range(4):
                    target[c, g, pl.ds(4 * t + j, count, stride=nr), :] = parts[j]

    def gather(source, count, target):
        for t in range(nr // 4):
            for c in range(2):
                parts = swap_blocks([source[c, pl.ds(4 * t + j, count, stride=nr), :] for j in range(4)])
                for i in range(nx):
                    target[i, t, pl.ds(c, count, stride=2), :] = parts[i]

    def joined(source, i, where):
        return jnp.concatenate([source[i, t, where] for t in range(nr // 4)], axis=1)

    field[...] = jnp.zeros_like(field)
    loads[0].wait()
    for r in range(nr):
        field[r * PAD : r * PAD + npt, :] = current_ref[r]
    loads[1].wait()
    send_a[...] = transform()
    pl.semaphore_wait(barrier, nf - 1 + nx - 1)
    each_group(lambda i, row, own: deliver(send_a, got_a, 0, recv_a.at[y], row, own))
    got_a[f] = send_a[f]
    loads[2].wait()
    for c in range(2):
        back[c] = jnp.swapaxes(refl[c], 0, 1)
    fill_window()

    def to_columns(i, row, own):
        arrived(got_a, nzc if own else nzc - 1, recv_a.at[row])
        holder, half = lax.div(row, 2), lax.rem(row, 2)

        @pl.when(holder != x)
        def _():
            message(
                got_a.at[part(row)], cols_a.at[x, part(half)], send_sem.at[1], recv_sem.at[1], (f, holder)
            )

    each_group_near(to_columns)
    cols_a[x] = got_a[part(x, nb)]
    arrived(send_a, nf - 1, send_sem.at[0])
    arrived(send_a, nb * (nx - 1), send_sem.at[1])
    arrived(send_a, nb * (nx - 1), recv_sem.at[1])

    spread(lambda i: cols_a[i], nb, weights, 0)
    real, imag = weights[0, 0].astype(BF16), weights[1, 0].astype(BF16)
    sums = dot(refl[0], jnp.concatenate([real, imag], axis=1), ((1,), (0,))) + dot(
        refl[1], jnp.concatenate([-imag, real], axis=1), ((1,), (0,))
    )
    partial[0], partial[1] = sums[:, :TILE], sums[:, TILE:]
    gather(partial, nf, blocks)

    def scatter(i, row, own):
        where = part(row, 2 * nzc)
        for step in range(1, nx):
            peer = lax.rem(x + step, nx)
            send_s[peer, where] = encode(joined(blocks, peer, where))
            message(
                send_s.at[peer, where], got_s.at[x, where], send_sem.at[2], recv_s.at[i], (f, peer)
            )

    each_group(scatter)

    def collect(i, row, own):
        where = part(row, 2 * nzc)
        arrived(got_s.at[0], 2 * nzc * (nx - 1), recv_s.at[i])
        total = joined(blocks, x, where)
        for step in range(1, nx):
            total = total + decode(got_s[lax.rem(x + step, nx), where])
        send_b[part(row)] = encode(total).reshape(nzc, 2, wide)
        deliver(send_b, got_b, 3, recv_sem.at[3], row, own)

    each_group(collect)
    got_b[f] = send_b[f]
    loads[3].wait()
    for i in range(nx - 1):
        arrived(send_s.at[0], rows, send_sem.at[2])
    arrived(send_b, nf - 1, send_sem.at[3])
    arrived(got_b, nf - 1, recv_sem.at[3])

    field[...] = invert(got_b[...]) * window[...]
    for r in range(nr):
        up_ref[r] = field[r * PAD : r * PAD + npt, :]

    send_c[...] = transform()
    each_group_near(lambda i, row, own: deliver(send_c, got_c, 4, recv_c.at[y], row, own))
    got_c[f] = send_c[f]

    def to_all(i, row, own):
        arrived(got_c, nzc if own else nzc - 1, recv_c.at[row])
        for step in range(1, nx):
            peer = lax.rem(x + step, nx)
            message(
                got_c.at[part(row)], all_c.at[x, part(row)], send_sem.at[5], recv_g.at[i], (f, peer)
            )
        all_c[x, part(row)] = got_c[part(row)]

    each_group_near(to_all)

    def take(i, row, own):
        arrived(got_c, nzc * (nx - 1), recv_g.at[i])
        spread(lambda s: all_c[s, part(row)], nzc, full, row)

    each_group_near(take)
    arrived(send_c, nf - 1, send_sem.at[4])
    for i in range(nx - 1):
        arrived(got_c, nf, send_sem.at[5])

    real, imag = full[0].reshape(nf * nr, TILE).astype(BF16), full[1].reshape(nf * nr, TILE).astype(BF16)
    sums = dot(back[0], jnp.concatenate([real, imag], axis=1), ((1,), (0,))) + dot(
        back[1], jnp.concatenate([imag, -real], axis=1), ((1,), (0,))
    )
    product[0], product[1] = sums[:, :TILE], sums[:, TILE:]
    gather(product, nb, stage)

    for step in (2, 1, 3, 0):
        peer = lax.rem(x + step, nx)
        send_e[peer] = encode(joined(stage, peer, pl.ds(0, 2 * nb))).reshape(nb, 2, wide)
        if step:
            message(send_e.at[peer], got_e.at[x], send_sem.at[6], recv_e.at[x], (f, peer))
    got_e[x] = send_e[x]
    for step in (0, 1, 3, 2):
        origin = lax.rem(x + step, nx)
        if step:
            arrived(got_e.at[0], nb, recv_e.at[origin])
        for half in range(2):
            row = 2 * origin + half

            def pass_on(peer):
                place = got_e.at[origin, peer - origin * nb]
                message(place, got_d.at[f], send_sem.at[7], recv_sem.at[7], (peer, x))

            members(row, pass_on, False)

            @pl.when(row != y)
            def _():
                pass_on(row * nzc + zc)

    got_d[f] = got_e[f // nb, lax.rem(f, nb)]
    loads[4].wait()
    for i in range(nx - 1):
        arrived(got_e.at[0], nb, send_sem.at[6])
    arrived(got_d, nf - 1, send_sem.at[7])
    arrived(got_d, nf - 1, recv_sem.at[7])
    signal = invert(got_d[...]) * window[...]
    for r in range(nr):
        down_ref[r] = direct_ref[r] + signal[r * PAD : r * PAD + npt]


def shards(nf, nx, direct, current, onsets, reflection):
    npt, nr, ntime = current.shape
    nb, wide = nf // nx, nr * PAD
    sources, columns = nf * nr, nb * nr
    forward, inverse = tables(nf, ntime)
    reflection = reflection.reshape(2, sources, columns)
    vmem = lambda shape, dtype: pltpu.VMEM(shape, dtype)
    scratch = [
        vmem((nr, npt, ntime), F32),
        vmem((nr, npt, ntime), F32),
        vmem((2, sources, columns), BF16),
        vmem((2, columns, sources), BF16),
        vmem((2, 2 * nf, ntime), BF16),
        vmem((2, 2 * nf, ntime), BF16),
        vmem((wide, ntime), F32),
        vmem((wide, ntime), F32),
        vmem((nf, 2, wide), BF16),
        vmem((nf, 2, wide), BF16),
        vmem((nx, nb, 2, wide), BF16),
        vmem((nx, nr // 4, 2 * nf, TILE), F32),
        vmem((2, 1, columns, TILE), F32),
        vmem((2, sources, TILE), F32),
        vmem((nx, nr // 4, 2 * nf, TILE), F32),
        vmem((nx, 2 * nf, wide), I16),
        vmem((nx, 2 * nf, wide), I16),
        vmem((nf, 2, wide), I16),
        vmem((nf, 2, wide), I16),
        vmem((nf, 2, wide), BF16),
        vmem((nf, 2, wide), BF16),
        vmem((nx, nf, 2, wide), BF16),
        vmem((2, 2 * nx, sources // (2 * nx), TILE), F32),
        vmem((2, columns, TILE), F32),
        vmem((nx, nb, 2, wide), I16),
        vmem((nx, nb, 2, wide), I16),
        vmem((nf, 2, wide), I16),
        pltpu.SemaphoreType.DMA((5,)),
        pltpu.SemaphoreType.DMA((8,)),
        pltpu.SemaphoreType.DMA((8,)),
        pltpu.SemaphoreType.DMA((2 * nx,)),
        pltpu.SemaphoreType.DMA((2 * nx,)),
        pltpu.SemaphoreType.DMA((2 * nx,)),
        pltpu.SemaphoreType.DMA((2 * nx,)),
        pltpu.SemaphoreType.DMA((nx,)),
    ]
    by_receiver = lambda a: jnp.swapaxes(a, 0, 1)
    hbm, inside = pl.BlockSpec(memory_space=pltpu.HBM), pl.BlockSpec(memory_space=pltpu.VMEM)
    out = pltpu.VMEM((nr, npt, ntime), F32)
    up, down = pl.pallas_call(
        functools.partial(kernel, (nf, nx, nr, npt)),
        out_shape=(out, out),
        in_specs=[hbm, hbm, inside, hbm, hbm, hbm],
        out_specs=(inside, inside),
        scratch_shapes=scratch,
        compiler_params=pltpu.CompilerParams(
            collective_id=0, has_side_effects=True, vmem_limit_bytes=63 * 1024 * 1024
        ),
        name="marchenko",
    )(
        by_receiver(direct), by_receiver(current), by_receiver(onsets),
        reflection, jnp.asarray(forward), jnp.asarray(inverse),
    )
    return by_receiver(up), by_receiver(down)


def solution(mesh):
    nf, nx = mesh.shape["freq"], mesh.shape["rows"]
    in_specs = (
        P("rows", "freq", None),
        P("rows", "freq", None),
        P("rows", "freq"),
        P(None, "freq", None, "rows"),
    )
    out_specs = (P("rows", "freq", None), P("rows", "freq", None))
    return jax.shard_map(
        functools.partial(shards, nf, nx), mesh=mesh, in_specs=in_specs, out_specs=out_specs, check_vma=False
    )
```

```python
import functools
import math

import jax
import jax.numpy as jnp
import ml_dtypes
import numpy as np
from jax import lax
from jax.experimental import pallas as pl
from jax.experimental.pallas import tpu as pltpu
from jax.sharding import PartitionSpec as P

MESH = pl.DeviceIdType.MESH
PART = 8
TILE = 128
PEAK = 32000.0
SPOT = 127
F32, BF16, I16 = jnp.float32, jnp.bfloat16, jnp.int16


def split(table):
    high = table.astype(ml_dtypes.bfloat16)
    low = (table - high.astype(np.float64)).astype(ml_dtypes.bfloat16)
    return np.stack([high, low])


def tables(nfreq, ntime):
    phase = (np.arange(nfreq)[:, None] * np.arange(ntime)[None, :] % ntime) * (2.0 * math.pi / ntime)
    weights = np.where(np.arange(nfreq) == 0, 1.0, 2.0)[:, None] / ntime
    forward = np.stack([np.cos(phase), -np.sin(phase)], axis=1)
    inverse = forward * weights[:, None]
    return (
        split(forward.reshape(2 * nfreq, ntime)),
        split(inverse.reshape(2 * nfreq, ntime)),
    )


def halves(value):
    high = value.astype(BF16)
    return high, (value - high.astype(F32)).astype(BF16)


def dot(a, b, contract):
    return lax.dot_general(a, b, (contract, ((), ())), preferred_element_type=F32)


def lanes(shape):
    return lax.broadcasted_iota(jnp.int32, shape, len(shape) - 1)


def turn(value, shift):
    return pltpu.roll(value, shift, len(value.shape) - 1)


def swap_blocks(arrays):
    arrays = list(arrays)
    lane = lanes(arrays[0].shape)
    for bit in (4, 2, 1):
        shift = PART * bit
        clear = (lane & shift) == 0
        for i in range(8):
            if not i & bit:
                a, b = arrays[i], arrays[i + bit]
                arrays[i] = jnp.where(clear, a, turn(b, shift))
                arrays[i + bit] = jnp.where(clear, turn(a, TILE - shift), b)
    return arrays


def encode(value):
    largest = jnp.max(jnp.abs(value), axis=1, keepdims=True)
    power = jnp.ceil(jnp.log2(jnp.maximum(largest, 1e-30)) + 1e-3)
    codes = jnp.round(value * (jnp.exp2(-power) * PEAK))
    return jnp.where(lanes(value.shape) == SPOT, power, codes).astype(jnp.int32).astype(I16)


def decode(codes):
    codes = codes.astype(jnp.int32).astype(F32)
    return codes * (jnp.exp2(codes[:, SPOT : SPOT + 1]) * (1.0 / PEAK))


def kernel(
    dims,
    direct_hbm, current_hbm, onsets_ref, reflection_hbm, forward_hbm, inverse_hbm,
    up_ref, down_ref,
    direct_ref, current_ref, refl, back, forward_ref, inverse_ref, field, window,
    send_a, got_a, cols_a, stage, weights,
    partial, blocks, mine, send_s, got_s, send_b, got_b,
    send_c, got_c, all_c, full, product,
    send_e, got_e, got_d,
    load_sem, send_sem, recv_a, recv_q, recv_s, recv_b, recv_c, recv_g, recv_e, recv_d,
):
    nf, nx, nr, npt = dims
    nb = nf // nx
    rows = 2 * nf
    chunks = npt // PART
    ny = 2 * nx
    nzc = nf // ny
    f, x = lax.axis_index("freq"), lax.axis_index("rows")
    y, zc = f // nzc, lax.rem(f, nzc)

    loads = [
        pltpu.make_async_copy(source, target, load_sem.at[i])
        for i, (source, target) in enumerate(
            [
                (current_hbm, current_ref),
                (forward_hbm, forward_ref),
                (reflection_hbm, refl),
                (inverse_hbm, inverse_ref),
                (direct_hbm, direct_ref),
            ]
        )
    ]
    for load in loads:
        load.start()

    def offset(count, i):
        if isinstance(i, int):
            return count // 2 + (i + 1) // 2 * (1 - 2 * (i % 2))
        return count // 2 + lax.div(i + 1, 2) * (1 - 2 * lax.rem(i, 2))

    def group(i):
        return lax.rem(y + offset(ny, i), ny)

    def members(row, act, own):
        for j in range(nzc - (not own)):
            act(row * nzc + lax.rem(zc + offset(nzc, j), nzc))

    def every(row, act):
        members(row, act, False)

        @pl.when(row != y)
        def _():
            act(row * nzc + zc)

    def each_group(act):
        def one(i, carry):
            act(i, group(i), True)
            return carry

        lax.fori_loop(0, ny - 1, one, 0)
        act(ny - 1, y, False)

    def each_group_near(act):
        act(ny - 1, y, False)

        def one(i, carry):
            act(ny - 1 - i, group(ny - 1 - i), True)
            return carry

        lax.fori_loop(1, ny, one, 0)

    def part(row, size=None):
        size = nzc if size is None else size
        return pl.ds(pl.multiple_of(row * size, size), size)

    barrier = pltpu.get_barrier_semaphore()

    def greet(peer):
        pl.semaphore_signal(barrier, inc=1, device_id=(peer, x), device_id_type=MESH)

    each_group(lambda i, row, own: members(row, greet, own))
    for step in range(1, nx):
        pl.semaphore_signal(barrier, inc=1, device_id=(f, lax.rem(x + step, nx)), device_id_type=MESH)

    def message(source, target, send, recv, peer):
        pltpu.make_async_remote_copy(
            src_ref=source, dst_ref=target, send_sem=send, recv_sem=recv, device_id=peer, device_id_type=MESH
        ).start()

    def deliver(source, target, send, recv, row, own):
        members(
            row,
            lambda peer: message(source.at[peer], target.at[f], send, recv, (peer, x)),
            own,
        )

    def arrived(ref, count, sem):
        pltpu.make_async_copy(ref.at[pl.ds(0, count)], ref.at[pl.ds(0, count)], sem).wait()

    def transform(ch):
        high, low = halves(field[ch])
        spectra = (
            dot(forward_ref[0], high, ((1,), (1,)))
            + dot(forward_ref[0], low, ((1,), (1,)))
            + dot(forward_ref[1], high, ((1,), (1,)))
        )
        return spectra.astype(BF16).reshape(nf, 2, TILE)

    def invert(messages):
        high, low = halves(decode(messages.reshape(rows, TILE)))
        return (
            dot(high, inverse_ref[0], ((0,), (0,)))
            + dot(low, inverse_ref[0], ((0,), (0,)))
            + dot(high, inverse_ref[1], ((0,), (0,)))
        )

    def fill_window():
        samples = lax.broadcasted_iota(jnp.int32, (npt, 2 * nf), 1).astype(F32)
        own = lax.broadcasted_iota(jnp.int32, (npt, npt), 0) == lax.broadcasted_iota(jnp.int32, (npt, npt), 1)
        window[...] = jnp.zeros_like(window)
        for r in range(nr):
            spread_out = jnp.where(own, onsets_ref[r : r + 1, :].astype(F32), 0.0)
            start = jnp.sum(spread_out, axis=1, keepdims=True)
            inside = (samples < start) | (samples > 2 * nf - start)
            kept = jnp.where(inside, 1.0, 0.0)
            for ch in range(chunks):
                window[ch, r * PART : (r + 1) * PART, :] = kept[ch * PART : (ch + 1) * PART]

    def each_chunk(act):
        def one(ch, carry):
            act(ch)
            return carry

        lax.fori_loop(0, chunks, one, 0)

    def points(ch):
        return pl.ds(pl.multiple_of(ch * PART, PART), PART)

    def spread(messages, count, target):
        for i in range(nx):
            stage[i, : 2 * count] = messages(i).reshape(2 * count, TILE).astype(F32)
        step = min(count, 32)
        for q in range(0, count, step):
            parts = swap_blocks(
                [stage[i, pl.ds(2 * q + c, step, stride=2), :] for c in range(2) for i in range(nx)]
            )
            for r in range(nr):
                part = parts[r] if r < 8 else turn(parts[r - 8], TILE // 2)
                target[pl.ds(q * nr + r, step, stride=nr), :] = part

    def gather(source, count, target):
        step = min(count, 32)
        for q in range(0, count, step):
            low = lanes((step, TILE)) < TILE // 2
            parts = [source[pl.ds(q * nr + r, step, stride=nr), :] for r in range(nr)]
            above = [turn(part, TILE // 2) for part in parts[8:]]
            above += [jnp.zeros((step, TILE), F32)] * (8 - len(above))
            parts = swap_blocks([jnp.where(low, a, b) for a, b in zip(parts[:8], above)])
            for c in range(2):
                for i in range(nx):
                    target[i, pl.ds(2 * q + c, step, stride=2), :] = parts[c * nx + i]

    def crossed(value, sign):
        low = lanes(value.shape) < TILE // 4
        return jnp.where(low, -sign * turn(value, TILE - TILE // 4), sign * turn(value, TILE // 4)).astype(BF16)

    field[...] = jnp.zeros_like(field)
    loads[0].wait()
    for r in range(nr):
        for ch in range(chunks):
            field[ch, r * PART : (r + 1) * PART, :] = current_ref[r, ch * PART : (ch + 1) * PART, :]
    loads[1].wait()

    def start_a(ch):
        send_a[ch] = transform(ch)

    each_chunk(start_a)
    pl.semaphore_wait(barrier, nf - 1 + nx - 1)

    def first(ch):
        each_group(
            lambda i, row, own: deliver(
                send_a.at[ch], got_a.at[ch], send_sem.at[0, ch], recv_a.at[ch, y], row, own
            )
        )
        got_a[ch, f] = send_a[ch, f]

    each_chunk(first)
    loads[2].wait()
    for c in range(2):
        back[c] = jnp.swapaxes(refl[c], 0, 1)
    fill_window()

    def columns(ch):
        def forward(i, row, own):
            arrived(got_a.at[ch], nzc if own else nzc - 1, recv_a.at[ch, row])
            holder, half = lax.div(row, 2), lax.rem(row, 2)

            @pl.when(holder != x)
            def _():
                message(
                    got_a.at[ch, part(row)], cols_a.at[ch, x, part(half)],
                    send_sem.at[1, ch], recv_q.at[ch], (f, holder),
                )

        each_group_near(forward)
        cols_a[ch, x] = got_a[ch, part(x, nb)]

    each_chunk(columns)

    def products(ch):
        arrived(got_a.at[0], nb * (nx - 1), recv_q.at[ch])
        spread(lambda i: cols_a[ch, i], nb, weights)
        value = weights[...]
        partial[...] = dot(refl[0], value.astype(BF16), ((1,), (0,))) + dot(
            refl[1], crossed(value, 1.0), ((1,), (0,))
        )
        gather(partial, nf, blocks)
        mine[ch] = blocks[x]
        for step in range(1, nx):
            peer = lax.rem(x + step, nx)
            send_s[ch, peer] = encode(blocks[peer])
        for away in (2, 1, 3, 0):
            place = lax.rem(f // nb + away, nx)
            where = part(place, 2 * nb)
            for step in (2, 1, 3):
                peer = lax.rem(x + step, nx)
                message(
                    send_s.at[ch, peer, where], got_s.at[ch, x, where],
                    send_sem.at[2, ch], recv_s.at[ch, away], (f, peer),
                )

    each_chunk(products)

    def collect(ch):
        for away in (2, 1, 3, 0):
            place = lax.rem(f // nb + away, nx)
            where = part(place, 2 * nb)
            arrived(got_s.at[0, 0], 2 * nb * (nx - 1), recv_s.at[ch, away])
            total = mine[ch, where]
            for step in range(1, nx):
                total = total + decode(got_s[ch, lax.rem(x + step, nx), where])
            send_b[ch, part(place, nb)] = encode(total).reshape(nb, 2, TILE)
            for half in range(2):
                every(
                    2 * place + half,
                    lambda peer: message(
                        send_b.at[ch, peer], got_b.at[ch, f], send_sem.at[3, ch], recv_b.at[ch], (peer, x)
                    ),
                )
        got_b[ch, f] = send_b[ch, f]

    each_chunk(collect)
    loads[3].wait()

    def upward(ch):
        arrived(got_b.at[ch], nf - 1, recv_b.at[ch])
        field[ch] = invert(got_b[ch]) * window[ch]
        send_c[ch] = transform(ch)
        each_group_near(
            lambda i, row, own: deliver(
                send_c.at[ch], got_c.at[ch], send_sem.at[4, ch], recv_c.at[ch, y], row, own
            )
        )
        got_c[ch, f] = send_c[ch, f]
        for r in range(nr):
            up_ref[r, points(ch), :] = field[ch, r * PART : (r + 1) * PART, :]

    each_chunk(upward)

    def to_all(ch):
        def forward(i, row, own):
            arrived(got_c.at[ch], nzc if own else nzc - 1, recv_c.at[ch, row])
            for step in (2, 1, 3):
                peer = lax.rem(x + step, nx)
                message(
                    got_c.at[ch, part(row)], all_c.at[ch, x, part(row)],
                    send_sem.at[5, ch], recv_g.at[ch], (f, peer),
                )

        each_group_near(forward)
        all_c[ch, x] = got_c[ch]

    each_chunk(to_all)

    def conjugate(ch):
        arrived(all_c.at[ch], nx - 1, recv_g.at[ch])
        spread(lambda i: all_c[ch, i], nf, full)
        value = full[...]
        product[...] = dot(back[0], value.astype(BF16), ((1,), (0,))) + dot(
            back[1], crossed(value, -1.0), ((1,), (0,))
        )
        gather(product, nb, stage)
        for step in (2, 1, 3, 0):
            peer = lax.rem(x + step, nx)
            send_e[ch, peer] = encode(stage[peer, : 2 * nb]).reshape(nb, 2, TILE)
            if step:
                message(send_e.at[ch, peer], got_e.at[ch, x], send_sem.at[6, ch], recv_e.at[ch, x], (f, peer))
        got_e[ch, x] = send_e[ch, x]

    def pass_on(ch, step):
        origin = lax.rem(x + step, nx)
        if step:
            arrived(got_e.at[0, 0], nb, recv_e.at[ch, origin])
        for half in range(2):
            every(
                2 * origin + half,
                lambda peer: message(
                    got_e.at[ch, origin, peer - origin * nb], got_d.at[ch, f],
                    send_sem.at[7, ch], recv_d.at[ch], (peer, x),
                ),
            )

    def others(ch):
        for step in (1, 3, 2):
            pass_on(ch, step)
        got_d[ch, f] = got_e[ch, f // nb, lax.rem(f, nb)]

    def backward(ch, carry):
        conjugate(ch)
        pass_on(ch, 0)

        @pl.when(ch > 0)
        def _():
            others(ch - 1)

        return carry

    lax.fori_loop(0, chunks, backward, 0)
    others(chunks - 1)
    loads[4].wait()

    def downward(ch):
        arrived(got_d.at[ch], nf - 1, recv_d.at[ch])
        signal = invert(got_d[ch]) * window[ch]
        for r in range(nr):
            down_ref[r, points(ch), :] = (
                direct_ref[r, points(ch), :] + signal[r * PART : (r + 1) * PART]
            )

    each_chunk(downward)

    def left(ch):
        for which, ref in ((0, send_a), (3, send_b), (4, send_c), (7, got_d)):
            arrived(ref.at[ch], nf - 1, send_sem.at[which, ch])
        for which in (1, 6):
            arrived(got_a.at[ch], nb * (nx - 1), send_sem.at[which, ch])
        arrived(send_s.at[ch], nx - 1, send_sem.at[2, ch])
        arrived(all_c.at[ch], nx - 1, send_sem.at[5, ch])

    each_chunk(left)


def shards(nf, nx, direct, current, onsets, reflection):
    npt, nr, ntime = current.shape
    nb, chunks = nf // nx, npt // PART
    sources, columns = nf * nr, nb * nr
    forward, inverse = tables(nf, ntime)
    reflection = reflection.reshape(2, sources, columns)
    vmem = lambda shape, dtype: pltpu.VMEM(shape, dtype)
    scratch = [
        vmem((nr, npt, ntime), F32),
        vmem((nr, npt, ntime), F32),
        vmem((2, sources, columns), BF16),
        vmem((2, columns, sources), BF16),
        vmem((2, 2 * nf, ntime), BF16),
        vmem((2, 2 * nf, ntime), BF16),
        vmem((chunks, TILE, ntime), F32),
        vmem((chunks, TILE, ntime), F32),
        vmem((chunks, nf, 2, TILE), BF16),
        vmem((chunks, nf, 2, TILE), BF16),
        vmem((chunks, nx, nb, 2, TILE), BF16),
        vmem((nx, 2 * nf, TILE), F32),
        vmem((columns, TILE), F32),
        vmem((sources, TILE), F32),
        vmem((nx, 2 * nf, TILE), F32),
        vmem((chunks, 2 * nf, TILE), F32),
        vmem((chunks, nx, 2 * nf, TILE), I16),
        vmem((chunks, nx, 2 * nf, TILE), I16),
        vmem((chunks, nf, 2, TILE), I16),
        vmem((chunks, nf, 2, TILE), I16),
        vmem((chunks, nf, 2, TILE), BF16),
        vmem((chunks, nf, 2, TILE), BF16),
        vmem((chunks, nx, nf, 2, TILE), BF16),
        vmem((sources, TILE), F32),
        vmem((columns, TILE), F32),
        vmem((chunks, nx, nb, 2, TILE), I16),
        vmem((chunks, nx, nb, 2, TILE), I16),
        vmem((chunks, nf, 2, TILE), I16),
        pltpu.SemaphoreType.DMA((5,)),
        pltpu.SemaphoreType.DMA((8, chunks)),
        pltpu.SemaphoreType.DMA((chunks, 2 * nx)),
        pltpu.SemaphoreType.DMA((chunks,)),
        pltpu.SemaphoreType.DMA((chunks, nx)),
        pltpu.SemaphoreType.DMA((chunks,)),
        pltpu.SemaphoreType.DMA((chunks, 2 * nx)),
        pltpu.SemaphoreType.DMA((chunks,)),
        pltpu.SemaphoreType.DMA((chunks, nx)),
        pltpu.SemaphoreType.DMA((chunks,)),
    ]
    by_receiver = lambda a: jnp.swapaxes(a, 0, 1)
    hbm, inside = pl.BlockSpec(memory_space=pltpu.HBM), pl.BlockSpec(memory_space=pltpu.VMEM)
    out = pltpu.VMEM((nr, npt, ntime), F32)
    up, down = pl.pallas_call(
        functools.partial(kernel, (nf, nx, nr, npt)),
        out_shape=(out, out),
        in_specs=[hbm, hbm, inside, hbm, hbm, hbm],
        out_specs=(inside, inside),
        scratch_shapes=scratch,
        compiler_params=pltpu.CompilerParams(
            collective_id=0, has_side_effects=True, vmem_limit_bytes=63 * 1024 * 1024
        ),
        name="marchenko",
    )(
        by_receiver(direct), by_receiver(current), by_receiver(onsets),
        reflection, jnp.asarray(forward), jnp.asarray(inverse),
    )
    return by_receiver(up), by_receiver(down)


def solution(mesh):
    nf, nx = mesh.shape["freq"], mesh.shape["rows"]
    in_specs = (
        P("rows", "freq", None),
        P("rows", "freq", None),
        P("rows", "freq"),
        P(None, "freq", None, "rows"),
    )
    out_specs = (P("rows", "freq", None), P("rows", "freq", None))
    return jax.shard_map(
        functools.partial(shards, nf, nx), mesh=mesh, in_specs=in_specs, out_specs=out_specs, check_vma=False
    )
```

```python
import functools
import math

import jax
import jax.numpy as jnp
import ml_dtypes
import numpy as np
from jax import lax
from jax.experimental import pallas as pl
from jax.experimental.pallas import tpu as pltpu
from jax.sharding import PartitionSpec as P

MESH = pl.DeviceIdType.MESH
PART = 8
TILE = 128
PEAK = 32000.0
SPOT = 127
F32, BF16, I16 = jnp.float32, jnp.bfloat16, jnp.int16


def split(table):
    high = table.astype(ml_dtypes.bfloat16)
    low = (table - high.astype(np.float64)).astype(ml_dtypes.bfloat16)
    return np.stack([high, low])


def tables(nfreq, ntime):
    phase = (np.arange(nfreq)[:, None] * np.arange(ntime)[None, :] % ntime) * (2.0 * math.pi / ntime)
    weights = np.where(np.arange(nfreq) == 0, 1.0, 2.0)[:, None] / ntime
    forward = np.stack([np.cos(phase), -np.sin(phase)], axis=1)
    inverse = forward * weights[:, None]
    return (
        split(forward.reshape(2 * nfreq, ntime)),
        split(inverse.reshape(2 * nfreq, ntime)),
    )


def halves(value):
    high = value.astype(BF16)
    return high, (value - high.astype(F32)).astype(BF16)


def dot(a, b, contract):
    return lax.dot_general(a, b, (contract, ((), ())), preferred_element_type=F32)


def lanes(shape):
    return lax.broadcasted_iota(jnp.int32, shape, len(shape) - 1)


def turn(value, shift):
    return pltpu.roll(value, shift, len(value.shape) - 1)


def swap_blocks(arrays):
    arrays = list(arrays)
    lane = lanes(arrays[0].shape)
    for bit in (4, 2, 1):
        shift = PART * bit
        clear = (lane & shift) == 0
        for i in range(8):
            if not i & bit:
                a, b = arrays[i], arrays[i + bit]
                arrays[i] = jnp.where(clear, a, turn(b, shift))
                arrays[i + bit] = jnp.where(clear, turn(a, TILE - shift), b)
    return arrays


def encode(value):
    largest = jnp.max(jnp.abs(value), axis=1, keepdims=True)
    power = jnp.ceil(jnp.log2(jnp.maximum(largest, 1e-30)) + 1e-3)
    codes = jnp.round(value * (jnp.exp2(-power) * PEAK))
    return jnp.where(lanes(value.shape) == SPOT, power, codes).astype(jnp.int32).astype(I16)


def decode(codes):
    codes = codes.astype(jnp.int32).astype(F32)
    return codes * (jnp.exp2(codes[:, SPOT : SPOT + 1]) * (1.0 / PEAK))


def kernel(
    dims,
    direct_hbm, current_hbm, onsets_ref, reflection_hbm, forward_hbm, inverse_hbm,
    up_ref, down_ref,
    direct_ref, current_ref, refl, back, forward_ref, inverse_ref, field, window,
    send_a, got_a, cols_a, stage, weights,
    partial, blocks, mine, send_s, got_s, send_b, got_b,
    send_c, got_c, all_c, full, product,
    send_e, got_e, got_d,
    load_sem, send_sem, recv_a, recv_q, recv_s, recv_b, recv_c, recv_g, recv_e, recv_d,
):
    nf, nx, nr, npt = dims
    nb = nf // nx
    rows = 2 * nf
    chunks = npt // PART
    ny = 2 * nx
    nzc = nf // ny
    f, x = lax.axis_index("freq"), lax.axis_index("rows")
    y, zc = f // nzc, lax.rem(f, nzc)

    loads = [
        pltpu.make_async_copy(source, target, load_sem.at[i])
        for i, (source, target) in enumerate(
            [
                (current_hbm, current_ref),
                (forward_hbm, forward_ref),
                (reflection_hbm, refl),
                (inverse_hbm, inverse_ref),
                (direct_hbm, direct_ref),
            ]
        )
    ]
    for load in loads:
        load.start()

    def offset(count, i):
        if isinstance(i, int):
            return count // 2 + (i + 1) // 2 * (1 - 2 * (i % 2))
        return count // 2 + lax.div(i + 1, 2) * (1 - 2 * lax.rem(i, 2))

    def group(i):
        return lax.rem(y + offset(ny, i), ny)

    def members(row, act, own):
        for j in range(nzc - (not own)):
            act(row * nzc + lax.rem(zc + offset(nzc, j), nzc))

    def every(row, act):
        members(row, act, False)

        @pl.when(row != y)
        def _():
            act(row * nzc + zc)

    def each_group(act):
        def one(i, carry):
            act(i, group(i), True)
            return carry

        lax.fori_loop(0, ny - 1, one, 0)
        act(ny - 1, y, False)

    def each_group_near(act):
        act(ny - 1, y, False)

        def one(i, carry):
            act(ny - 1 - i, group(ny - 1 - i), True)
            return carry

        lax.fori_loop(1, ny, one, 0)

    def part(row, size=None):
        size = nzc if size is None else size
        return pl.ds(pl.multiple_of(row * size, size), size)

    barrier = pltpu.get_barrier_semaphore()

    def greet(peer):
        pl.semaphore_signal(barrier, inc=1, device_id=(peer, x), device_id_type=MESH)

    each_group(lambda i, row, own: members(row, greet, own))
    for step in range(1, nx):
        pl.semaphore_signal(barrier, inc=1, device_id=(f, lax.rem(x + step, nx)), device_id_type=MESH)

    def message(source, target, send, recv, peer):
        pltpu.make_async_remote_copy(
            src_ref=source, dst_ref=target, send_sem=send, recv_sem=recv, device_id=peer, device_id_type=MESH
        ).start()

    def deliver(source, target, send, recv, row, own):
        members(
            row,
            lambda peer: message(source.at[peer], target.at[f], send, recv, (peer, x)),
            own,
        )

    def arrived(ref, count, sem):
        pltpu.make_async_copy(ref.at[pl.ds(0, count)], ref.at[pl.ds(0, count)], sem).wait()

    def transform(ch):
        high, low = halves(field[ch])
        spectra = (
            dot(forward_ref[0], high, ((1,), (1,)))
            + dot(forward_ref[0], low, ((1,), (1,)))
            + dot(forward_ref[1], high, ((1,), (1,)))
        )
        return spectra.astype(BF16).reshape(nf, 2, TILE)

    def invert(messages):
        high, low = halves(decode(messages.reshape(rows, TILE)))
        return (
            dot(high, inverse_ref[0], ((0,), (0,)))
            + dot(low, inverse_ref[0], ((0,), (0,)))
            + dot(high, inverse_ref[1], ((0,), (0,)))
        )

    def fill_window():
        samples = lax.broadcasted_iota(jnp.int32, (npt, 2 * nf), 1).astype(F32)
        own = lax.broadcasted_iota(jnp.int32, (npt, npt), 0) == lax.broadcasted_iota(jnp.int32, (npt, npt), 1)
        window[...] = jnp.zeros_like(window)
        for r in range(nr):
            spread_out = jnp.where(own, onsets_ref[r : r + 1, :].astype(F32), 0.0)
            start = jnp.sum(spread_out, axis=1, keepdims=True)
            inside = (samples < start) | (samples > 2 * nf - start)
            kept = jnp.where(inside, 1.0, 0.0)
            for ch in range(chunks):
                window[ch, r * PART : (r + 1) * PART, :] = kept[ch * PART : (ch + 1) * PART]

    def each_chunk(act):
        def one(ch, carry):
            act(ch)
            return carry

        lax.fori_loop(0, chunks, one, 0)

    def points(ch):
        return pl.ds(pl.multiple_of(ch * PART, PART), PART)

    def spread(messages, count, target):
        for i in range(nx):
            stage[i, : 2 * count] = messages(i).reshape(2 * count, TILE).astype(F32)
        step = min(count, 32)
        for q in range(0, count, step):
            parts = swap_blocks(
                [stage[i, pl.ds(2 * q + c, step, stride=2), :] for c in range(2) for i in range(nx)]
            )
            for r in range(nr):
                part = parts[r] if r < 8 else turn(parts[r - 8], TILE // 2)
                target[pl.ds(q * nr + r, step, stride=nr), :] = part

    def gather(source, count, target):
        step = min(count, 32)
        for q in range(0, count, step):
            low = lanes((step, TILE)) < TILE // 2
            parts = [source[pl.ds(q * nr + r, step, stride=nr), :] for r in range(nr)]
            above = [turn(part, TILE // 2) for part in parts[8:]]
            above += [jnp.zeros((step, TILE), F32)] * (8 - len(above))
            parts = swap_blocks([jnp.where(low, a, b) for a, b in zip(parts[:8], above)])
            for c in range(2):
                for i in range(nx):
                    target[i, pl.ds(2 * q + c, step, stride=2), :] = parts[c * nx + i]

    def crossed(value, sign):
        low = lanes(value.shape) < TILE // 4
        return jnp.where(low, -sign * turn(value, TILE - TILE // 4), sign * turn(value, TILE // 4)).astype(BF16)

    field[...] = jnp.zeros_like(field)
    loads[0].wait()
    for r in range(nr):
        for ch in range(chunks):
            field[ch, r * PART : (r + 1) * PART, :] = current_ref[r, ch * PART : (ch + 1) * PART, :]
    loads[1].wait()

    def start_a(ch):
        send_a[ch] = transform(ch)

    each_chunk(start_a)
    pl.semaphore_wait(barrier, nf - 1 + nx - 1)

    def first(ch):
        each_group(
            lambda i, row, own: deliver(
                send_a.at[ch], got_a.at[ch], send_sem.at[0, ch], recv_a.at[ch, y], row, own
            )
        )
        got_a[ch, f] = send_a[ch, f]

    each_chunk(first)
    loads[2].wait()
    for c in range(2):
        back[c] = jnp.swapaxes(refl[c], 0, 1)
    fill_window()

    def columns(ch):
        def forward(i, row, own):
            arrived(got_a.at[ch], nzc if own else nzc - 1, recv_a.at[ch, row])
            holder, half = lax.div(row, 2), lax.rem(row, 2)

            @pl.when(holder != x)
            def _():
                message(
                    got_a.at[ch, part(row)], cols_a.at[ch, x, part(half)],
                    send_sem.at[1, ch], recv_q.at[ch], (f, holder),
                )

        each_group_near(forward)
        cols_a[ch, x] = got_a[ch, part(x, nb)]

    each_chunk(columns)

    def products(ch):
        arrived(got_a.at[0], nb * (nx - 1), recv_q.at[ch])
        spread(lambda i: cols_a[ch, i], nb, weights)
        value = weights[...]
        partial[...] = dot(refl[0], value.astype(BF16), ((1,), (0,))) + dot(
            refl[1], crossed(value, 1.0), ((1,), (0,))
        )
        gather(partial, nf, blocks)
        mine[ch] = blocks[x]
        for step in range(1, nx):
            peer = lax.rem(x + step, nx)
            send_s[ch, peer] = encode(blocks[peer])
        for away in (2, 1, 3, 0):
            place = lax.rem(f // nb + away, nx)
            where = part(place, 2 * nb)
            for step in (2, 1, 3):
                peer = lax.rem(x + step, nx)
                message(
                    send_s.at[ch, peer, where], got_s.at[ch, x, where],
                    send_sem.at[2, ch], recv_s.at[ch, away], (f, peer),
                )

    each_chunk(products)

    def collect(ch):
        for away in (2, 1, 3, 0):
            place = lax.rem(f // nb + away, nx)
            where = part(place, 2 * nb)
            arrived(got_s.at[0, 0], 2 * nb * (nx - 1), recv_s.at[ch, away])
            total = mine[ch, where]
            for step in range(1, nx):
                total = total + decode(got_s[ch, lax.rem(x + step, nx), where])
            send_b[ch, part(place, nb)] = encode(total).reshape(nb, 2, TILE)
            for half in range(2):
                every(
                    2 * place + half,
                    lambda peer: message(
                        send_b.at[ch, peer], got_b.at[ch, f], send_sem.at[3, ch], recv_b.at[ch], (peer, x)
                    ),
                )
        got_b[ch, f] = send_b[ch, f]

    each_chunk(collect)
    loads[3].wait()

    def upward(ch):
        arrived(got_b.at[ch], nf - 1, recv_b.at[ch])
        field[ch] = invert(got_b[ch]) * window[ch]
        send_c[ch] = transform(ch)
        each_group(
            lambda i, row, own: deliver(
                send_c.at[ch], got_c.at[ch], send_sem.at[4, ch], recv_c.at[ch, y], row, own
            )
        )
        got_c[ch, f] = send_c[ch, f]
        for r in range(nr):
            up_ref[r, points(ch), :] = field[ch, r * PART : (r + 1) * PART, :]

    each_chunk(upward)

    def to_all(ch):
        def forward(i, row, own):
            arrived(got_c.at[ch], nzc if own else nzc - 1, recv_c.at[ch, row])
            for step in (2, 1, 3):
                peer = lax.rem(x + step, nx)
                message(
                    got_c.at[ch, part(row)], all_c.at[ch, x, part(row)],
                    send_sem.at[5, ch], recv_g.at[ch], (f, peer),
                )

        each_group_near(forward)
        all_c[ch, x] = got_c[ch]

    each_chunk(to_all)

    def conjugate(ch):
        arrived(all_c.at[ch], nx - 1, recv_g.at[ch])
        spread(lambda i: all_c[ch, i], nf, full)
        value = full[...]
        product[...] = dot(back[0], value.astype(BF16), ((1,), (0,))) + dot(
            back[1], crossed(value, -1.0), ((1,), (0,))
        )
        gather(product, nb, stage)
        for step in (2, 1, 3, 0):
            peer = lax.rem(x + step, nx)
            send_e[ch, peer] = encode(stage[peer, : 2 * nb]).reshape(nb, 2, TILE)
            if step:
                message(send_e.at[ch, peer], got_e.at[ch, x], send_sem.at[6, ch], recv_e.at[ch, x], (f, peer))
        got_e[ch, x] = send_e[ch, x]

    def pass_on(ch, step):
        origin = lax.rem(x + step, nx)
        if step:
            arrived(got_e.at[0, 0], nb, recv_e.at[ch, origin])
        for half in range(2):
            every(
                2 * origin + half,
                lambda peer: message(
                    got_e.at[ch, origin, peer - origin * nb], got_d.at[ch, f],
                    send_sem.at[7, ch], recv_d.at[ch], (peer, x),
                ),
            )

    def others(ch):
        for step in (1, 3, 2):
            pass_on(ch, step)
        got_d[ch, f] = got_e[ch, f // nb, lax.rem(f, nb)]

    def backward(ch, carry):
        conjugate(ch)
        pass_on(ch, 0)

        @pl.when(ch > 0)
        def _():
            others(ch - 1)

        return carry

    lax.fori_loop(0, chunks, backward, 0)
    others(chunks - 1)
    loads[4].wait()

    def downward(ch):
        arrived(got_d.at[ch], nf - 1, recv_d.at[ch])
        signal = invert(got_d[ch]) * window[ch]
        for r in range(nr):
            down_ref[r, points(ch), :] = (
                direct_ref[r, points(ch), :] + signal[r * PART : (r + 1) * PART]
            )

    each_chunk(downward)

    def left(ch):
        for which, ref in ((0, send_a), (3, send_b), (4, send_c), (7, got_d)):
            arrived(ref.at[ch], nf - 1, send_sem.at[which, ch])
        for which in (1, 6):
            arrived(got_a.at[ch], nb * (nx - 1), send_sem.at[which, ch])
        arrived(send_s.at[ch], nx - 1, send_sem.at[2, ch])
        arrived(all_c.at[ch], nx - 1, send_sem.at[5, ch])

    each_chunk(left)


def shards(nf, nx, direct, current, onsets, reflection):
    npt, nr, ntime = current.shape
    nb, chunks = nf // nx, npt // PART
    sources, columns = nf * nr, nb * nr
    forward, inverse = tables(nf, ntime)
    reflection = reflection.reshape(2, sources, columns)
    vmem = lambda shape, dtype: pltpu.VMEM(shape, dtype)
    scratch = [
        vmem((nr, npt, ntime), F32),
        vmem((nr, npt, ntime), F32),
        vmem((2, sources, columns), BF16),
        vmem((2, columns, sources), BF16),
        vmem((2, 2 * nf, ntime), BF16),
        vmem((2, 2 * nf, ntime), BF16),
        vmem((chunks, TILE, ntime), F32),
        vmem((chunks, TILE, ntime), F32),
        vmem((chunks, nf, 2, TILE), BF16),
        vmem((chunks, nf, 2, TILE), BF16),
        vmem((chunks, nx, nb, 2, TILE), BF16),
        vmem((nx, 2 * nf, TILE), F32),
        vmem((columns, TILE), F32),
        vmem((sources, TILE), F32),
        vmem((nx, 2 * nf, TILE), F32),
        vmem((chunks, 2 * nf, TILE), F32),
        vmem((chunks, nx, 2 * nf, TILE), I16),
        vmem((chunks, nx, 2 * nf, TILE), I16),
        vmem((chunks, nf, 2, TILE), I16),
        vmem((chunks, nf, 2, TILE), I16),
        vmem((chunks, nf, 2, TILE), BF16),
        vmem((chunks, nf, 2, TILE), BF16),
        vmem((chunks, nx, nf, 2, TILE), BF16),
        vmem((sources, TILE), F32),
        vmem((columns, TILE), F32),
        vmem((chunks, nx, nb, 2, TILE), I16),
        vmem((chunks, nx, nb, 2, TILE), I16),
        vmem((chunks, nf, 2, TILE), I16),
        pltpu.SemaphoreType.DMA((5,)),
        pltpu.SemaphoreType.DMA((8, chunks)),
        pltpu.SemaphoreType.DMA((chunks, 2 * nx)),
        pltpu.SemaphoreType.DMA((chunks,)),
        pltpu.SemaphoreType.DMA((chunks, nx)),
        pltpu.SemaphoreType.DMA((chunks,)),
        pltpu.SemaphoreType.DMA((chunks, 2 * nx)),
        pltpu.SemaphoreType.DMA((chunks,)),
        pltpu.SemaphoreType.DMA((chunks, nx)),
        pltpu.SemaphoreType.DMA((chunks,)),
    ]
    by_receiver = lambda a: jnp.swapaxes(a, 0, 1)
    hbm, inside = pl.BlockSpec(memory_space=pltpu.HBM), pl.BlockSpec(memory_space=pltpu.VMEM)
    out = pltpu.VMEM((nr, npt, ntime), F32)
    up, down = pl.pallas_call(
        functools.partial(kernel, (nf, nx, nr, npt)),
        out_shape=(out, out),
        in_specs=[hbm, hbm, inside, hbm, hbm, hbm],
        out_specs=(inside, inside),
        scratch_shapes=scratch,
        compiler_params=pltpu.CompilerParams(
            collective_id=0, has_side_effects=True, vmem_limit_bytes=63 * 1024 * 1024
        ),
        name="marchenko",
    )(
        by_receiver(direct), by_receiver(current), by_receiver(onsets),
        reflection, jnp.asarray(forward), jnp.asarray(inverse),
    )
    return by_receiver(up), by_receiver(down)


def solution(mesh):
    nf, nx = mesh.shape["freq"], mesh.shape["rows"]
    in_specs = (
        P("rows", "freq", None),
        P("rows", "freq", None),
        P("rows", "freq"),
        P(None, "freq", None, "rows"),
    )
    out_specs = (P("rows", "freq", None), P("rows", "freq", None))
    return jax.shard_map(
        functools.partial(shards, nf, nx), mesh=mesh, in_specs=in_specs, out_specs=out_specs, check_vma=False
    )
```
